128 devices in a mesh: dp: 4 (over x), pipe: 2 (over core), tensor: 16 (over z, y).
Axes of the slice: x: 4, y: 4, z: 4, core: 2. Of those that a mesh axis runs over, the one named last changes fastest.
Arguments:
- queries: bfloat16 [8, 34, 16384], P(('dp', 'pipe')), parts along dimension 0, may hold values from -80 to 80
- cache_k: bfloat16 [8, 3, 32768, 1024], P(('dp', 'pipe'), None, 'tensor'), parts along dimension 0, may hold values from -4 to 4
- cache_v: bfloat16 [8, 3, 32768, 1024], P(('dp', 'pipe'), None, 'tensor'), parts along dimension 0, may hold values from -6 to 6
- dec_lengths: int32 [8, 2], P(('dp', 'pipe')), parts along dimension 0, may hold values from 2 to 32768, as said below
- pre_starts: int32 [8], P(('dp', 'pipe')), parts along dimension 0, may hold values from 0 to 32736, as said below
Outputs:
- handed: bfloat16 [8, 34, 16384], P(('dp', 'pipe'), None, 'tensor'), parts along dimension 0
The draws below stay inside these ranges and needn't reach their ends.
There are 4 independent parts, one for each index of `dp`. The reference program is written for one: setup_inputs(seed, part) draws one part's arguments, and reference() takes and returns one part's arrays. A program takes and returns all parts, laid end to end along the dimension named above; each array names one. Nothing has to cross between parts.
Inputs may be any that keep to these rules, and one draw needn't show every extreme that they name: `dec_lengths`: every decode row has at least two live positions; some row of some section uses all 32768 positions. `pre_starts`: every prefill block fits in the cache; some section's block ends at the last position.
All inputs are finite; a program needn't handle non-finite values.
Results may differ from the reference program's by a relative error of at most 0.0075.
Values may be sent and summed in bfloat16 or wider, within the bound.
No kernel may reach another device: no remote copies, remote signals or barrier semaphores. Data moves between devices by JAX's collectives and lax.ppermute only.
A program may use at most 192 MiB of HBM per device.

```python
import math
import jax
import jax.numpy as jnp
from jax import lax

HQ = 128
KVH = 8
HD = 128
DEC = 2
PRE = 32
CT_DEV = 2048
CACHE = 32768
SECTIONS = 2


def shared_lengths(key):
    key = jax.random.fold_in(key, 7)
    count = SECTIONS * DEC
    lengths = jax.random.randint(key, (count,), 2, CACHE + 1)
    chosen_spot = jax.random.randint(jax.random.fold_in(key, 1), (), 0, count)
    lengths = lengths.at[chosen_spot].set(CACHE)
    lengths = lengths.at[(chosen_spot + 1) % count].set(2)
    return lengths.reshape(SECTIONS, DEC).astype(jnp.int32)


def shared_starts(key):
    key = jax.random.fold_in(key, 9)
    starts = jax.random.randint(key, (SECTIONS,), 0, CACHE - PRE + 1)
    chosen_spot = jax.random.randint(jax.random.fold_in(key, 1), (), 0, SECTIONS)
    starts = starts.at[chosen_spot].set(CACHE - PRE)
    return starts.astype(jnp.int32)


def draw_cache_k(key, part):
    key = jax.random.fold_in(key, 3)
    blocks = CACHE // CT_DEV
    drawn = jax.random.normal(jax.random.fold_in(key, 1), (SECTIONS, DEC + 1, blocks, CT_DEV, KVH, HD), jnp.float32)
    factor = jnp.exp(jax.random.uniform(jax.random.fold_in(key, 2), (SECTIONS, DEC + 1, blocks, 1, KVH, 1), jnp.float32, -0.55, 0.55))
    table = jnp.clip(drawn * factor, -4.0, 4.0).reshape(SECTIONS, DEC + 1, CACHE, KVH * HD)
    return table.astype(jnp.bfloat16)


def draw_queries(key, part):
    key = jax.random.fold_in(key, 5)
    drawn = jnp.clip(jax.random.normal(key, (SECTIONS, DEC + PRE, HQ * HD), jnp.float32), -4.0, 4.0)
    rows = jnp.arange(DEC + PRE)
    loud = (rows == DEC - 1) | (rows >= DEC + PRE - 5) & (rows <= DEC + PRE - 2)
    drawn = drawn * jnp.where(loud, 5.0, 1.0)[None, :, None]
    return drawn.astype(jnp.bfloat16)


def draw_dec_lengths(key, part):
    lengths = shared_lengths(key)
    return lengths


def draw_pre_starts(key, part):
    starts = shared_starts(key)
    return starts


def steps_of(key, shape, pieces, low, top_value):
    level, own = 1.0, jax.random.fold_in(key, 6)
    for axis_at, shards_of in pieces:
        draws = jnp.exp(jax.random.uniform(jax.random.fold_in(own, axis_at), (shards_of,), jnp.float32, low / len(pieces), top_value / len(pieces)))
        level = level * jnp.repeat(draws, shape[axis_at] // shards_of).reshape([-1 if axis == axis_at else 1 for axis in range(len(shape))])
    return level


def centred(stream_key, extent, deviation, most, pieces=(), held_as=jnp.bfloat16):
    loudness = steps_of(stream_key, extent, pieces, -0.22, 0.18) if pieces else 1.0
    result = jax.random.normal(stream_key, extent, jnp.float32) * deviation * loudness
    return jnp.minimum(jnp.maximum(result, -most), most).astype(held_as)


def setup_inputs(seed: int = 0, part: int = 0) -> dict:
    keys = jax.random.split(jax.random.key(seed), 6)
    part_keys = jax.random.split(jax.random.fold_in(keys[5], part), 6)
    return {
        "queries": draw_queries(jax.random.fold_in(jax.random.fold_in(keys[5], part), 71), part),
        "cache_k": draw_cache_k(jax.random.fold_in(jax.random.fold_in(keys[5], part), 71), part),
        "cache_v": centred(part_keys[2], (SECTIONS, DEC + 1, CACHE, KVH * HD), 1.0, 6.0, ((0, 2), (2, 16))),
        "dec_lengths": draw_dec_lengths(jax.random.fold_in(jax.random.fold_in(keys[5], part), 71), part),
        "pre_starts": draw_pre_starts(jax.random.fold_in(jax.random.fold_in(keys[5], part), 71), part),
    }


NEGATIVE_FILL = -1e+30

def attend(scores, live, values, form):
    maxima = lax.optimization_barrier(jnp.max(jnp.where(live, scores, NEGATIVE_FILL), axis=-1))
    weights = jnp.where(live, jnp.exp(scores - maxima[..., None]), 0.0)
    totals = lax.optimization_barrier(jnp.sum(weights, axis=-1))
    rounded = lax.optimization_barrier(weights.astype(jnp.bfloat16)).astype(jnp.float32)
    summed = jnp.einsum(form, rounded, values)
    return summed / totals[..., None]

def reference(queries, cache_k, cache_v, dec_lengths, pre_starts):
    group_size = HQ // KVH
    softmax_scale = 1.0 / math.sqrt(HD)
    positions = jnp.arange(CACHE, dtype=jnp.int32)
    tokens_pre = jnp.arange(PRE, dtype=jnp.int32)

    def one_section(section_args):
        query_rows, key_cache, value_cache, lengths, span_start = section_args
        query_rows = query_rows.astype(jnp.float32)
        key_cache = key_cache.astype(jnp.float32)
        value_cache = value_cache.astype(jnp.float32)
        dec_query = query_rows[:DEC].reshape(DEC, KVH, group_size, HD)
        dec_keys = key_cache[:DEC].reshape(DEC, CACHE, KVH, HD)
        dec_values = value_cache[:DEC].reshape(DEC, CACHE, KVH, HD)
        dec_scores = jnp.einsum('bkgd,bpkd->bkgp', dec_query, dec_keys) * softmax_scale
        live_dec = (positions[None, :] < lengths[:, None])[:, None, None, :]
        dec_out = attend(dec_scores, live_dec, dec_values, 'bkgp,bpkd->bkgd')
        pre_query = query_rows[DEC:].reshape(PRE, KVH, group_size, HD)
        pre_keys = key_cache[DEC].reshape(CACHE, KVH, HD)
        pre_values = value_cache[DEC].reshape(CACHE, KVH, HD)
        pre_scores = jnp.einsum('qkgd,pkd->qkgp', pre_query, pre_keys) * softmax_scale
        live_pre = (positions[None, :] <= span_start + tokens_pre[:, None])[:, None, None, :]
        pre_out = attend(pre_scores, live_pre, pre_values, 'qkgp,pkd->qkgd')
        joined = jnp.concatenate([dec_out.reshape(DEC, HQ * HD), pre_out.reshape(PRE, HQ * HD)], 0)
        return joined.astype(jnp.bfloat16)
    attended = lax.map(one_section, (queries, cache_k, cache_v, dec_lengths, pre_starts))
    return jnp.roll(attended, 1, axis=0)
```

```python
import math

import jax
import jax.numpy as jnp
from jax import lax
from jax.experimental import pallas as pl
from jax.experimental.pallas import tpu as pltpu
from jax.sharding import PartitionSpec as P

HQ = 128
KVH = 8
HD = 128
GROUP = HQ // KVH
HALF = GROUP // 2
DEC = 2
PRE = 32
LANES = GROUP * PRE
TILE = 512
ROWS = 160
SCALE = math.log2(math.e) / math.sqrt(HD)
DEAD = -1e30
FLOOR = -1e29


def three_parts(x):
    first = x.astype(jnp.bfloat16).astype(jnp.float32)
    rest = x - first
    second = rest.astype(jnp.bfloat16).astype(jnp.float32)
    return first, second, rest - second


def nt_dot(a, b):
    return lax.dot_general(a, b, (((1,), (1,)), ((), ())), preferred_element_type=jnp.float32)


def tn_dot(a, b):
    return lax.dot_general(a, b, (((0,), (0,)), ((), ())), preferred_element_type=jnp.float32)


def attend_kernel(scalars, q_ref, k_ref, v_ref, out_ref):
    local_len = k_ref.shape[1]
    offset = scalars[0]
    start = scalars[1]
    rows = q_ref[...].astype(jnp.float32)
    pre_rows = rows[DEC:]
    pre_query = jnp.concatenate(
        [pre_rows[:, g * HD : (g + 1) * HD] for g in range(GROUP)], 0
    ).astype(jnp.bfloat16)

    def prefill(masked):
        token = lax.broadcasted_iota(jnp.int32, (1, LANES), 1) % PRE
        limit = start + token - offset
        top = jnp.full((1, LANES), FLOOR, jnp.float32)
        total = jnp.zeros((1, LANES), jnp.float32)
        acc = jnp.zeros((HD, LANES), jnp.float32)
        for tile in range(local_len // TILE):
            span = slice(tile * TILE, (tile + 1) * TILE)
            scores = nt_dot(k_ref[DEC, span], pre_query) * SCALE
            if masked:
                place = lax.broadcasted_iota(jnp.int32, (TILE, LANES), 0) + tile * TILE
                scores = jnp.where(place <= limit, scores, DEAD)
            new_top = jnp.maximum(top, jnp.max(scores, axis=0, keepdims=True))
            weights = jnp.exp2(scores - new_top)
            factor = jnp.exp2(top - new_top)
            total = total * factor + jnp.sum(weights, axis=0, keepdims=True)
            acc = acc * factor + tn_dot(v_ref[DEC, span], weights.astype(jnp.bfloat16))
            top = new_top
        stats = [*three_parts(top), *three_parts(total)]
        stats.append(jnp.zeros((2, LANES), jnp.float32))
        stats = jnp.concatenate(stats, 0)
        for j in range(2):
            lanes = slice(j * LANES // 2, (j + 1) * LANES // 2)
            out_ref[j, :HD, :] = acc[:, lanes].astype(jnp.bfloat16)
        return stats

    def decode():
        place = lax.broadcasted_iota(jnp.int32, (GROUP, local_len), 1)
        lane = lax.broadcasted_iota(jnp.int32, (GROUP, HD), 1)
        weighted, packed = [], []
        for b in range(DEC):
            query = jnp.concatenate(
                [rows[b : b + 1, g * HD : (g + 1) * HD] for g in range(GROUP)], 0
            ).astype(jnp.bfloat16)
            scores = nt_dot(query, k_ref[b]) * SCALE
            scores = jnp.where(place < scalars[2 + b] - offset, scores, DEAD)
            top = jnp.maximum(jnp.max(scores, axis=1, keepdims=True), FLOOR)
            weights = jnp.exp2(scores - top)
            total = jnp.sum(weights, axis=1, keepdims=True)
            weighted.append(
                jnp.dot(weights.astype(jnp.bfloat16), v_ref[b], preferred_element_type=jnp.float32)
            )
            stats = jnp.zeros((GROUP, HD), jnp.float32)
            for place_of, part in enumerate([*three_parts(top), *three_parts(total)]):
                stats = jnp.where(lane == place_of, part, stats)
            packed.append(stats)
        return jnp.concatenate(weighted, 1), jnp.concatenate(packed, 1)

    def finish(pre_stats):
        dec_weighted, dec_stats = decode()
        for j in range(2):
            heads = slice(j * HALF, (j + 1) * HALF)
            lanes = slice(j * LANES // 2, (j + 1) * LANES // 2)
            tail = jnp.concatenate(
                [
                    dec_weighted[heads],
                    pre_stats[:, lanes],
                    dec_stats[heads],
                    jnp.zeros((8, LANES // 2), jnp.float32),
                ],
                0,
            )
            out_ref[j, HD:, :] = tail.astype(jnp.bfloat16)

    whole = offset + local_len - 1 <= start

    @pl.when(whole)
    def _():
        finish(prefill(False))

    @pl.when(jnp.logical_not(whole))
    def _():
        finish(prefill(True))


def attend(scalars, queries, cache_k, cache_v):
    rows = queries.shape[0]
    sequences, local_len, _ = cache_k.shape
    return pl.pallas_call(
        attend_kernel,
        grid_spec=pltpu.PrefetchScalarGridSpec(
            num_scalar_prefetch=1,
            grid=(KVH,),
            in_specs=[
                pl.BlockSpec((rows, GROUP * HD), lambda h, s: (0, h)),
                pl.BlockSpec((sequences, local_len, HD), lambda h, s: (0, 0, h)),
                pl.BlockSpec((sequences, local_len, HD), lambda h, s: (0, 0, h)),
            ],
            out_specs=pl.BlockSpec((2, ROWS, LANES // 2), lambda h, s: (h, 0, 0)),
        ),
        out_shape=jax.ShapeDtypeStruct((2 * KVH, ROWS, LANES // 2), jnp.bfloat16),
        compiler_params=pltpu.CompilerParams(vmem_limit_bytes=48 * 1024 * 1024),
        name="attend",
    )(scalars, queries, cache_k, cache_v)


def join_kernel(parts_ref, out_ref):
    sources = parts_ref.shape[0]

    def stats_of(j, row):
        return parts_ref[j, HD:, :].astype(jnp.float32)[row : row + 8]

    pre_tops, pre_totals, dec_tops, dec_totals = [], [], [], []
    for j in range(sources):
        pre = stats_of(j, 8)
        pre_tops.append(pre[0:1] + pre[1:2] + pre[2:3])
        pre_totals.append(pre[3:4] + pre[4:5] + pre[5:6])
        dec = stats_of(j, 16)
        for tops, at in ((dec_tops, 0), (dec_totals, 3)):
            tops.append(
                [
                    sum(dec[:, b * HD + at + n : b * HD + at + n + 1] for n in range(3))
                    for b in range(DEC)
                ]
            )
    top = pre_tops[0]
    for other in pre_tops[1:]:
        top = jnp.maximum(top, other)
    total = jnp.zeros_like(top)
    acc = jnp.zeros((HD, LANES // 2), jnp.float32)
    for j in range(sources):
        factor = jnp.exp2(pre_tops[j] - top)
        total += factor * pre_totals[j]
        acc += factor * parts_ref[j, :HD, :].astype(jnp.float32)
    joined = (acc / total).T
    pre_out = jnp.concatenate([joined[g * PRE : (g + 1) * PRE] for g in range(HALF)], 1)
    dec_out = []
    for b in range(DEC):
        top = dec_tops[0][b]
        for other in dec_tops[1:]:
            top = jnp.maximum(top, other[b])
        total = jnp.zeros_like(top)
        acc = jnp.zeros((HALF, HD), jnp.float32)
        for j in range(sources):
            factor = jnp.exp2(dec_tops[j][b] - top)
            total += factor * dec_totals[j][b]
            acc += factor * stats_of(j, 0)[:, b * HD : (b + 1) * HD]
        joined = acc / total
        dec_out.append(jnp.concatenate([joined[g : g + 1] for g in range(HALF)], 1))
    out_ref[...] = jnp.concatenate([*dec_out, pre_out], 0).astype(jnp.bfloat16)


def join(parts):
    return pl.pallas_call(
        join_kernel,
        out_shape=jax.ShapeDtypeStruct((DEC + PRE, HALF * HD), jnp.bfloat16),
        in_specs=[pl.BlockSpec(memory_space=pltpu.VMEM)],
        out_specs=pl.BlockSpec(memory_space=pltpu.VMEM),
        compiler_params=pltpu.CompilerParams(vmem_limit_bytes=32 * 1024 * 1024),
        name="join",
    )(parts)


def on_device(queries, cache_k, cache_v, dec_lengths, pre_starts):
    local_len = cache_k.shape[2]
    offset = lax.axis_index("tensor") * local_len
    scalars = jnp.concatenate([offset[None], pre_starts, dec_lengths[0]]).astype(jnp.int32)
    parts = attend(scalars, queries[0], cache_k[0], cache_v[0])
    parts = lax.all_to_all(parts, "tensor", 0, 0, tiled=True)
    own_share = join(parts)
    count = lax.axis_size("pipe")
    pairs = [(source, (source + 1) % count) for source in range(count)]
    handed = lax.ppermute(own_share, "pipe", pairs)
    return handed[None]


def solution(mesh):
    in_specs = (
        P(("dp", "pipe"), None, None),
        P(("dp", "pipe"), None, "tensor", None),
        P(("dp", "pipe"), None, "tensor", None),
        P(("dp", "pipe"), None),
        P(("dp", "pipe")),
    )
    out_specs = P(("dp", "pipe"), None, "tensor")
    return jax.shard_map(
        on_device, mesh=mesh, in_specs=in_specs, out_specs=out_specs, check_vma=False
    )
```

```python
import functools
import math

import jax
import jax.numpy as jnp
from jax import lax
from jax.experimental import pallas as pl
from jax.experimental.pallas import tpu as pltpu
from jax.sharding import PartitionSpec as P

HQ = 128
KVH = 8
HD = 128
GROUP = HQ // KVH
ACROSS = 4
HALF = GROUP // 2
DEC = 2
PRE = 32
LANES = GROUP * PRE
PAIR = 2
QK_TILE = 512
PV_TILE = 1024
ROWS = 160
SCALE = math.log2(math.e) / math.sqrt(HD)
DEAD = -1e30
FLOOR = -1e29
VMEM_LIMIT = 36 * 1024 * 1024
FETCHED = ("q", "k", "n", "v", "k0", "v0", "k1", "v1")
FIRST_SCHEDULE = "A0A1AA" "xBa0Ba0B0B" "Wb01b01" "111"
SCHEDULE = "A0A1AA" "Ba0Ba0B0B" "b01b01" "111"


def three_parts(x):
    first = x.astype(jnp.bfloat16).astype(jnp.float32)
    rest = x - first
    second = rest.astype(jnp.bfloat16).astype(jnp.float32)
    return first, second, rest - second


def nt_dot(a, b):
    return lax.dot_general(a, b, (((1,), (1,)), ((), ())), preferred_element_type=jnp.float32)


def tn_dot(a, b):
    return lax.dot_general(a, b, (((0,), (0,)), ((), ())), preferred_element_type=jnp.float32)


def scores_of(keys, query, s_ref, limit):
    local_len = keys.shape[0]
    top = jnp.full((1, LANES), FLOOR, jnp.float32)
    for at in range(0, local_len, QK_TILE):
        block = keys[at : at + QK_TILE]
        scores = nt_dot(jnp.concatenate([block, block], 1), query)
        if limit is not None:
            place = lax.broadcasted_iota(jnp.int32, (QK_TILE, LANES), 0) + at
            scores = jnp.where(place <= limit, scores, DEAD)
        s_ref[at : at + QK_TILE] = scores
        top = jnp.maximum(top, jnp.max(scores, axis=0, keepdims=True))
        yield top


def weighted_of(values, s_ref, top_of):
    local_len = values.shape[0]
    top = top_of()
    acc = None
    for at in range(0, local_len, PV_TILE):
        weights = jnp.exp2(s_ref[at : at + PV_TILE] - top).astype(jnp.bfloat16)
        block = jnp.concatenate(
            [values[at : at + PV_TILE].T, jnp.ones((16, PV_TILE), jnp.bfloat16)], 0
        )
        part = jnp.dot(block, weights, preferred_element_type=jnp.float32)
        acc = part if acc is None else acc + part
        yield acc


def decode_of(b, rows, k_ref, v_ref, length):
    local_len = k_ref.shape[1]
    blank = jnp.zeros((GROUP, HD), jnp.float32)
    query = []
    for n in range(PAIR):
        part = jnp.concatenate(
            [rows[b : b + 1, (n * GROUP + g) * HD : (n * GROUP + g + 1) * HD] for g in range(GROUP)], 0
        )
        query.append(jnp.concatenate([part if n == m else blank for m in range(PAIR)], 1))
    query = jnp.concatenate(query, 0).astype(jnp.bfloat16)
    yield
    scores = nt_dot(query, k_ref[b]) * SCALE
    yield
    place = lax.broadcasted_iota(jnp.int32, (GROUP * PAIR, local_len), 1)
    scores = jnp.where(place < length, scores, DEAD)
    top = jnp.maximum(jnp.max(scores, axis=1, keepdims=True), FLOOR)
    yield
    weights = jnp.exp2(scores - top)
    total = jnp.sum(weights, axis=1, keepdims=True)
    yield
    both = jnp.dot(weights.astype(jnp.bfloat16), v_ref[b], preferred_element_type=jnp.float32)
    yield
    weighted = jnp.concatenate(
        [both[n * GROUP : (n + 1) * GROUP, n * HD : (n + 1) * HD] for n in range(PAIR)], 0
    )
    yield weighted, top, total


def place_of_device():
    place = lax.axis_index("tensor")
    return lax.axis_index("pipe"), place // ACROSS, place % ACROSS


def moved(here, by):
    return lax.rem(here + by, ACROSS)


def fetches(shift, sources, targets, sems):
    section, slow, _ = place_of_device()
    pair = moved(slow, jnp.where(section == 0, shift[0], shift[1]))
    q_hbm, k_hbm, v_hbm = sources
    q_ref, k_ref, v_ref = targets

    def columns(count):
        return pl.ds(pl.multiple_of(pair * count, count), count)

    moves = {"q": (q_hbm.at[:, columns(PAIR * GROUP * HD)], q_ref)}
    for name, sequence in (("", DEC), *((str(b), b) for b in range(DEC))):
        for kind, hbm, ref in (("k", k_hbm, k_ref), ("v", v_hbm, v_ref)):
            moves[kind + name] = (hbm.at[sequence, :, columns(PAIR * HD)], ref.at[sequence])
    return {
        name: pltpu.make_async_copy(*move, sems.at[n]) for n, (name, move) in enumerate(moves.items())
    }


def attend_kernel(shift, after, *refs):
    refs = list(refs)

    def take(count):
        return [refs.pop(0) for _ in range(count)]

    first = shift == ORDER[0]
    (starts,) = take(1)
    if first:
        (lengths_hbm,) = take(1)
    else:
        (lengths_ref,) = take(1)
        held = take(3)
    sources = take(3) if first or after is not None else None
    (out_ref,) = take(1)
    if first:
        (lengths_ref,) = take(1)
    coming = take(3) if after is not None else None
    s_first, s_second, sems, later_sems = take(4)
    if first:
        lengths, *held = take(4)
    q_ref, k_ref, v_ref = held
    local_len = k_ref.shape[1]
    offset = lax.axis_index("tensor") * local_len

    waiting = {}
    if first:
        waiting = fetches(shift, sources, held, sems)
        waiting["n"] = pltpu.make_async_copy(lengths_hbm, lengths, sems.at[len(waiting)])
        for name in FETCHED:
            waiting[name].start()
    later = fetches(after, sources, coming, later_sems) if after is not None else {}

    def start_later():
        for copy in later.values():
            copy.start()

    if not first:
        start_later()

    @pl.when(starts[0] >= 0)
    def _():
        def wait(names):
            for name in names:
                if name in waiting:
                    waiting.pop(name).wait()

        wait(("q",))
        rows = q_ref[...].astype(jnp.float32)
        pre_rows = rows[DEC:] * SCALE
        queries = []
        for n in range(PAIR):
            query = jnp.concatenate(
                [pre_rows[:, (n * GROUP + g) * HD : (n * GROUP + g + 1) * HD] for g in range(GROUP)], 0
            )
            high = query.astype(jnp.bfloat16)
            low = (query - high.astype(jnp.float32)).astype(jnp.bfloat16)
            queries.append(jnp.concatenate([high, low], 1))
        wait(("n", "k"))
        if first:
            start_later()
        token = lax.broadcasted_iota(jnp.int32, (1, LANES), 1) % PRE
        limit = starts[0] + token - offset
        if first:
            row = lax.broadcasted_iota(jnp.int32, lengths_ref.shape, 0)
            lengths_ref[...] = functools.reduce(
                lambda rest, b: jnp.where(row == b, lengths[0, b], rest), range(DEC), jnp.zeros_like(row)
            )

        def keys(n):
            return k_ref.at[DEC, :, n * HD : (n + 1) * HD]

        def values(n):
            return v_ref.at[DEC, :, n * HD : (n + 1) * HD]

        last = {}
        streams = {
            "A": scores_of(keys(0), queries[0], s_first, limit),
            "B": scores_of(keys(1), queries[1], s_second, limit),
            "a": weighted_of(values(0), s_first, lambda: last["A"]),
            "b": weighted_of(values(1), s_second, lambda: last["B"]),
        }
        for b in range(DEC):
            length = lengths[0, b] if first else lengths_ref[b : b + 1, 0:1]
            streams[str(b)] = decode_of(b, rows, k_ref, v_ref, length - offset)
        for name in FIRST_SCHEDULE if first else SCHEDULE:
            if name == "x":
                wait(("v", "k0"))
            elif name == "W":
                wait(list(waiting))
            else:
                last[name] = next(streams[name])
        dec_first, dec_second = last["0"], last["1"]
        top_first, acc_first, top_second, acc_second = (last[name] for name in "AaBb")
        for n, (top, acc) in enumerate(((top_first, acc_first), (top_second, acc_second))):
            for j in range(2):
                heads = slice(n * GROUP + j * HALF, n * GROUP + (j + 1) * HALF)
                lanes = slice(j * LANES // 2, (j + 1) * LANES // 2)
                out_ref[2 * n + j] = packed(
                    acc[:HD, lanes],
                    top[:, lanes],
                    acc[HD : HD + 1, lanes],
                    [[part[heads] for part in one] for one in (dec_first, dec_second)],
                )
    for copy in later.values():
        copy.wait()


def packed(acc, top, total, dec):
    lane = lax.broadcasted_iota(jnp.int32, (HALF, HD), 1)
    dec_stats = []
    for _, dec_top, dec_total in dec:
        stats = jnp.zeros((HALF, HD), jnp.float32)
        for place_of, part in enumerate([*three_parts(dec_top), *three_parts(dec_total)]):
            stats = jnp.where(lane == place_of, part, stats)
        dec_stats.append(stats)
    return jnp.concatenate(
        [
            acc,
            jnp.concatenate([one[0] for one in dec], 1),
            *three_parts(top),
            *three_parts(total),
            jnp.zeros((2, LANES // 2), jnp.float32),
            jnp.concatenate(dec_stats, 1),
            jnp.zeros((8, LANES // 2), jnp.float32),
        ],
        0,
    ).astype(jnp.bfloat16)


def attend(shift, after, starts, lengths, held, sources):
    first = shift == ORDER[0]
    queries, cache_k, _ = sources
    rows = queries.shape[0]
    sequences, local_len, _ = cache_k.shape
    operands = [
        ((rows, PAIR * GROUP * HD), queries.dtype),
        ((sequences, local_len, PAIR * HD), cache_k.dtype),
        ((sequences, local_len, PAIR * HD), cache_k.dtype),
    ]
    args = [starts, lengths, *held]
    in_specs = [pl.BlockSpec(memory_space=pltpu.SMEM)]
    in_specs += [pl.BlockSpec(memory_space=pl.ANY if first else pltpu.VMEM)] * (1 + len(held))
    if first or after is not None:
        args += sources
        in_specs += [pl.BlockSpec(memory_space=pl.ANY)] * 3
    outs = [pltpu.VMEM((ACROSS, ROWS, LANES // 2), jnp.bfloat16)]
    if first:
        outs.append(pltpu.VMEM((8, HD), jnp.int32))
    if after is not None:
        outs += [pltpu.VMEM(*operand) for operand in operands]
    scratch = [
        pltpu.VMEM((local_len, LANES), jnp.float32),
        pltpu.VMEM((local_len, LANES), jnp.float32),
        pltpu.SemaphoreType.DMA((2 * sequences + 2,)),
        pltpu.SemaphoreType.DMA((2 * sequences + 2,)),
    ]
    if first:
        scratch.append(pltpu.SMEM(lengths.shape, jnp.int32))
        scratch += [pltpu.VMEM(*operand) for operand in operands]
    part, *rest = pl.pallas_call(
        functools.partial(attend_kernel, shift, after),
        in_specs=in_specs,
        out_specs=[pl.BlockSpec(memory_space=pltpu.VMEM)] * len(outs),
        out_shape=outs,
        scratch_shapes=scratch,
        compiler_params=pltpu.CompilerParams(vmem_limit_bytes=VMEM_LIMIT),
        cost_estimate=pl.CostEstimate(
            flops=4 * PAIR * GROUP * HD * (PRE + DEC) * local_len,
            bytes_accessed=4 * sequences * local_len * PAIR * HD,
            transcendentals=PAIR * GROUP * (PRE + DEC) * local_len,
        ),
        name="attend",
    )(*args)
    if first:
        lengths, *rest = rest
    return part, lengths, rest


def joined(parts):
    def add(tops, totals, sums):
        top = functools.reduce(jnp.maximum, tops)
        factors = [jnp.exp2(one - top) for one in tops]
        total = sum(factor * one for factor, one in zip(factors, totals))
        return sum(factor * one for factor, one in zip(factors, sums)), top, total

    tails = [part[HD:, :].astype(jnp.float32) for part in parts]
    stats = [tail[8:16] for tail in tails]
    pre = add(
        [one[0:1] + one[1:2] + one[2:3] for one in stats],
        [one[3:4] + one[4:5] + one[5:6] for one in stats],
        [part[:HD, :].astype(jnp.float32) for part in parts],
    )
    dec = []
    for b in range(DEC):
        at = b * HD
        stats = [tail[16:24] for tail in tails]
        dec.append(
            add(
                [sum(one[:, at + n : at + n + 1] for n in range(3)) for one in stats],
                [sum(one[:, at + n : at + n + 1] for n in range(3, 6)) for one in stats],
                [tail[:8, at : at + HD] for tail in tails],
            )
        )
    return pre, dec


def join_some_kernel(*refs):
    parts, outs = refs[:ACROSS], refs[ACROSS:]
    _, _, fast = place_of_device()
    for by, out in zip(FAST_ORDER, outs):
        target = moved(fast, by)
        pre, dec = joined([part.at[target] for part in parts])
        out[...] = packed(*pre, dec)


def join_some(parts):
    return pl.pallas_call(
        join_some_kernel,
        in_specs=[pl.BlockSpec(memory_space=pltpu.VMEM)] * ACROSS,
        out_specs=[pl.BlockSpec(memory_space=pltpu.VMEM)] * ACROSS,
        out_shape=[jax.ShapeDtypeStruct((ROWS, LANES // 2), jnp.bfloat16)] * ACROSS,
        compiler_params=pltpu.CompilerParams(vmem_limit_bytes=32 * 1024 * 1024),
        name="join_some",
    )(*parts)


def join_last_kernel(*refs):
    (acc, _, total), dec = joined(refs[:-1])
    result = (acc / total).T
    rows = []
    for dec_acc, _, dec_total in dec:
        one = dec_acc / dec_total
        rows.append(jnp.concatenate([one[g : g + 1] for g in range(HALF)], 1))
    rows.append(jnp.concatenate([result[g * PRE : (g + 1) * PRE] for g in range(HALF)], 1))
    refs[-1][...] = jnp.concatenate(rows, 0).astype(jnp.bfloat16)


def join_last(parts):
    return pl.pallas_call(
        join_last_kernel,
        in_specs=[pl.BlockSpec(memory_space=pltpu.VMEM)] * ACROSS,
        out_specs=pl.BlockSpec(memory_space=pltpu.VMEM),
        out_shape=jax.ShapeDtypeStruct((DEC + PRE, HALF * HD), jnp.bfloat16),
        compiler_params=pltpu.CompilerParams(vmem_limit_bytes=32 * 1024 * 1024),
        name="join_last",
    )(*parts)


def sent(value, step):
    sections = lax.axis_size("pipe")
    pairs = []
    for section in range(sections):
        by_section, by_slow, by_fast = step(section)
        to_section = (section + by_section) % sections
        for slow in range(ACROSS):
            for fast in range(ACROSS):
                to = ((slow + by_slow) % ACROSS) * ACROSS + (fast + by_fast) % ACROSS
                here = (section * ACROSS + slow) * ACROSS + fast
                pairs.append((here, to_section * ACROSS * ACROSS + to))
    return lax.ppermute(value, ("pipe", "tensor"), pairs)


ORDER = ((2, 2), (3, 1), (1, 3), (0, 0))
FAST_ORDER = (2, 1, 3, 0)


def on_device(queries, cache_k, cache_v, dec_lengths, pre_starts):
    sources = [
        pltpu.with_memory_space_constraint(one, pltpu.HBM) for one in (queries[0], cache_k[0], cache_v[0])
    ]
    lengths = pltpu.with_memory_space_constraint(dec_lengths, pltpu.HBM)
    held, parts = [], []
    for shift, after in zip(ORDER, (*ORDER[1:], None)):
        part, lengths, held = attend(shift, after, pre_starts, lengths, held, sources)
        if shift != (0, 0):
            part = sent(part, lambda section, shift=shift: (0, shift[section % 2], 0))
        parts.append(part)
    shares = join_some(parts)
    shares = [sent(share, lambda section, by=by: (1, 0, by)) for by, share in zip(FAST_ORDER, shares)]
    return join_last(shares)[None]


def solution(mesh):
    in_specs = (
        P(("dp", "pipe"), None, None),
        P(("dp", "pipe"), None, "tensor", None),
        P(("dp", "pipe"), None, "tensor", None),
        P(("dp", "pipe"), None),
        P(("dp", "pipe")),
    )
    out_specs = P(("dp", "pipe"), None, "tensor")
    return jax.shard_map(
        on_device, mesh=mesh, in_specs=in_specs, out_specs=out_specs, check_vma=False
    )
```

```python
import functools
import math

import jax
import jax.numpy as jnp
from jax import lax
from jax.experimental import pallas as pl
from jax.experimental.pallas import tpu as pltpu
from jax.sharding import PartitionSpec as P

HQ = 128
KVH = 8
HD = 128
GROUP = HQ // KVH
ACROSS = 4
HALF = GROUP // 2
DEC = 2
PRE = 32
LANES = GROUP * PRE
PAIR = 2
QK_TILE = 512
PV_TILE = 1024
ROWS = 144
SCALE = math.log2(math.e) / math.sqrt(HD)
DEAD = -1e30
FLOOR = -1e29
VMEM_LIMIT = 36 * 1024 * 1024
FETCHED = ("q", "k", "n", "v", "k0", "v0", "k1", "v1")
FIRST_SCHEDULE = "A0A1AA" "xBa0Ba0B0B" "Wb01b01" "111"
SCHEDULE = "A0A1AA" "Ba0Ba0B0B" "b01b01" "111"


def three_parts(x):
    first = x.astype(jnp.bfloat16).astype(jnp.float32)
    rest = x - first
    second = rest.astype(jnp.bfloat16).astype(jnp.float32)
    return first, second, rest - second


def nt_dot(a, b):
    return lax.dot_general(a, b, (((1,), (1,)), ((), ())), preferred_element_type=jnp.float32)


def tn_dot(a, b):
    return lax.dot_general(a, b, (((0,), (0,)), ((), ())), preferred_element_type=jnp.float32)


def scores_of(keys, query, s_ref, limit):
    local_len = keys.shape[0]
    top = jnp.full((1, LANES), FLOOR, jnp.float32)
    for at in range(0, local_len, QK_TILE):
        block = keys[at : at + QK_TILE]
        scores = nt_dot(jnp.concatenate([block, block], 1), query)
        if limit is not None:
            place = lax.broadcasted_iota(jnp.int32, (QK_TILE, LANES), 0) + at
            scores = jnp.where(place <= limit, scores, DEAD)
        s_ref[at : at + QK_TILE] = scores
        top = jnp.maximum(top, jnp.max(scores, axis=0, keepdims=True))
        yield top


def weighted_of(values, s_ref, top_of):
    local_len = values.shape[0]
    top = top_of()
    acc = None
    for at in range(0, local_len, PV_TILE):
        weights = jnp.exp2(s_ref[at : at + PV_TILE] - top).astype(jnp.bfloat16)
        block = jnp.concatenate(
            [values[at : at + PV_TILE].T, jnp.ones((16, PV_TILE), jnp.bfloat16)], 0
        )
        part = jnp.dot(block, weights, preferred_element_type=jnp.float32)
        acc = part if acc is None else acc + part
        yield acc


def decode_of(b, rows, k_ref, v_ref, length):
    local_len = k_ref.shape[1]
    blank = jnp.zeros((GROUP, HD), jnp.float32)
    query = []
    for n in range(PAIR):
        part = jnp.concatenate(
            [rows[b : b + 1, (n * GROUP + g) * HD : (n * GROUP + g + 1) * HD] for g in range(GROUP)], 0
        )
        query.append(jnp.concatenate([part if n == m else blank for m in range(PAIR)], 1))
    query = jnp.concatenate(query, 0).astype(jnp.bfloat16)
    yield
    scores = nt_dot(query, k_ref[b]) * SCALE
    yield
    place = lax.broadcasted_iota(jnp.int32, (GROUP * PAIR, local_len), 1)
    scores = jnp.where(place < length, scores, DEAD)
    top = jnp.maximum(jnp.max(scores, axis=1, keepdims=True), FLOOR)
    yield
    weights = jnp.exp2(scores - top)
    total = jnp.sum(weights, axis=1, keepdims=True)
    yield
    both = jnp.dot(weights.astype(jnp.bfloat16), v_ref[b], preferred_element_type=jnp.float32)
    yield
    weighted = jnp.concatenate(
        [both[n * GROUP : (n + 1) * GROUP, n * HD : (n + 1) * HD] for n in range(PAIR)], 0
    )
    yield weighted, top, total


def place_of_device():
    place = lax.axis_index("tensor")
    return lax.axis_index("pipe"), place // ACROSS, place % ACROSS


def moved(here, by):
    return lax.rem(here + by, ACROSS)


def fetches(shift, sources, targets, sems):
    section, slow, _ = place_of_device()
    pair = moved(slow, jnp.where(section == 0, shift[0], shift[1]))
    q_hbm, k_hbm, v_hbm = sources
    q_ref, k_ref, v_ref = targets

    def columns(count):
        return pl.ds(pl.multiple_of(pair * count, count), count)

    moves = {"q": (q_hbm.at[:, columns(PAIR * GROUP * HD)], q_ref)}
    for name, sequence in (("", DEC), *((str(b), b) for b in range(DEC))):
        for kind, hbm, ref in (("k", k_hbm, k_ref), ("v", v_hbm, v_ref)):
            moves[kind + name] = (hbm.at[sequence, :, columns(PAIR * HD)], ref.at[sequence])
    return {
        name: pltpu.make_async_copy(*move, sems.at[n]) for n, (name, move) in enumerate(moves.items())
    }


def attend_kernel(shift, after, *refs):
    refs = list(refs)

    def take(count):
        return [refs.pop(0) for _ in range(count)]

    first = shift == ORDER[0]
    (starts,) = take(1)
    if first:
        (lengths_hbm,) = take(1)
    else:
        (lengths_ref,) = take(1)
        held = take(3)
    sources = take(3) if first or after is not None else None
    (out_ref,) = take(1)
    if first:
        (lengths_ref,) = take(1)
    coming = take(3) if after is not None else None
    s_first, s_second, sems, later_sems = take(4)
    if first:
        lengths, *held = take(4)
    q_ref, k_ref, v_ref = held
    local_len = k_ref.shape[1]
    offset = lax.axis_index("tensor") * local_len

    waiting = {}
    if first:
        waiting = fetches(shift, sources, held, sems)
        waiting["n"] = pltpu.make_async_copy(lengths_hbm, lengths, sems.at[len(waiting)])
        for name in FETCHED:
            waiting[name].start()
    later = fetches(after, sources, coming, later_sems) if after is not None else {}

    def start_later():
        for copy in later.values():
            copy.start()

    if not first:
        start_later()

    @pl.when(starts[0] >= 0)
    def _():
        def wait(names):
            for name in names:
                if name in waiting:
                    waiting.pop(name).wait()

        wait(("q",))
        rows = q_ref[...].astype(jnp.float32)
        pre_rows = rows[DEC:] * SCALE
        queries = []
        for n in range(PAIR):
            query = jnp.concatenate(
                [pre_rows[:, (n * GROUP + g) * HD : (n * GROUP + g + 1) * HD] for g in range(GROUP)], 0
            )
            high = query.astype(jnp.bfloat16)
            low = (query - high.astype(jnp.float32)).astype(jnp.bfloat16)
            queries.append(jnp.concatenate([high, low], 1))
        wait(("n", "k"))
        if first:
            start_later()
        token = lax.broadcasted_iota(jnp.int32, (1, LANES), 1) % PRE
        limit = starts[0] + token - offset
        if first:
            row = lax.broadcasted_iota(jnp.int32, lengths_ref.shape, 0)
            lengths_ref[...] = functools.reduce(
                lambda rest, b: jnp.where(row == b, lengths[0, b], rest), range(DEC), jnp.zeros_like(row)
            )

        def keys(n):
            return k_ref.at[DEC, :, n * HD : (n + 1) * HD]

        def values(n):
            return v_ref.at[DEC, :, n * HD : (n + 1) * HD]

        last = {}
        streams = {
            "A": scores_of(keys(0), queries[0], s_first, limit),
            "B": scores_of(keys(1), queries[1], s_second, limit),
            "a": weighted_of(values(0), s_first, lambda: last["A"]),
            "b": weighted_of(values(1), s_second, lambda: last["B"]),
        }
        for b in range(DEC):
            length = lengths[0, b] if first else lengths_ref[b : b + 1, 0:1]
            streams[str(b)] = decode_of(b, rows, k_ref, v_ref, length - offset)
        for name in FIRST_SCHEDULE if first else SCHEDULE:
            if name == "x":
                wait(("v", "k0"))
            elif name == "W":
                wait(list(waiting))
            else:
                last[name] = next(streams[name])
        dec_first, dec_second = last["0"], last["1"]
        top_first, acc_first, top_second, acc_second = (last[name] for name in "AaBb")
        for n, (top, acc) in enumerate(((top_first, acc_first), (top_second, acc_second))):
            for j in range(2):
                heads = slice(n * GROUP + j * HALF, n * GROUP + (j + 1) * HALF)
                lanes = slice(j * LANES // 2, (j + 1) * LANES // 2)
                out_ref[2 * n + j] = packed(
                    acc[:HD, lanes],
                    top[:, lanes],
                    acc[HD : HD + 1, lanes],
                    [[part[heads] for part in one] for one in (dec_first, dec_second)],
                )
    for copy in later.values():
        copy.wait()


def packed(acc, top, total, dec):
    dec_stats = []
    for _, dec_top, dec_total in dec:
        parts = [*three_parts(dec_top), *three_parts(dec_total)]
        stats = sum(jnp.where(in_lanes(n), part, 0.0) for n, part in enumerate(parts))
        dec_stats.append(jnp.sum(stats, axis=0, keepdims=True))
    return jnp.concatenate(
        [
            acc,
            jnp.concatenate([one[0] for one in dec], 1),
            *three_parts(top),
            *three_parts(total),
            jnp.concatenate(dec_stats, 1),
            jnp.zeros((1, LANES // 2), jnp.float32),
        ],
        0,
    ).astype(jnp.bfloat16)


def in_lanes(n):
    row = lax.broadcasted_iota(jnp.int32, (HALF, HD), 0)
    return lax.broadcasted_iota(jnp.int32, (HALF, HD), 1) == n * HALF + row


def attend(shift, after, starts, lengths, held, sources):
    first = shift == ORDER[0]
    queries, cache_k, _ = sources
    rows = queries.shape[0]
    sequences, local_len, _ = cache_k.shape
    operands = [
        ((rows, PAIR * GROUP * HD), queries.dtype),
        ((sequences, local_len, PAIR * HD), cache_k.dtype),
        ((sequences, local_len, PAIR * HD), cache_k.dtype),
    ]
    args = [starts, lengths, *held]
    in_specs = [pl.BlockSpec(memory_space=pltpu.SMEM)]
    in_specs += [pl.BlockSpec(memory_space=pl.ANY if first else pltpu.VMEM)] * (1 + len(held))
    if first or after is not None:
        args += sources
        in_specs += [pl.BlockSpec(memory_space=pl.ANY)] * 3
    outs = [pltpu.VMEM((ACROSS, ROWS, LANES // 2), jnp.bfloat16)]
    if first:
        outs.append(pltpu.VMEM((8, HD), jnp.int32))
    if after is not None:
        outs += [pltpu.VMEM(*operand) for operand in operands]
    scratch = [
        pltpu.VMEM((local_len, LANES), jnp.float32),
        pltpu.VMEM((local_len, LANES), jnp.float32),
        pltpu.SemaphoreType.DMA((2 * sequences + 2,)),
        pltpu.SemaphoreType.DMA((2 * sequences + 2,)),
    ]
    if first:
        scratch.append(pltpu.SMEM(lengths.shape, jnp.int32))
        scratch += [pltpu.VMEM(*operand) for operand in operands]
    part, *rest = pl.pallas_call(
        functools.partial(attend_kernel, shift, after),
        in_specs=in_specs,
        out_specs=[pl.BlockSpec(memory_space=pltpu.VMEM)] * len(outs),
        out_shape=outs,
        scratch_shapes=scratch,
        compiler_params=pltpu.CompilerParams(vmem_limit_bytes=VMEM_LIMIT),
        cost_estimate=pl.CostEstimate(
            flops=4 * PAIR * GROUP * HD * (PRE + DEC) * local_len,
            bytes_accessed=4 * sequences * local_len * PAIR * HD,
            transcendentals=PAIR * GROUP * (PRE + DEC) * local_len,
        ),
        name="attend",
    )(*args)
    if first:
        lengths, *rest = rest
    return part, lengths, rest


def joined(parts):
    def add(tops, totals, sums):
        top = functools.reduce(jnp.maximum, tops)
        factors = [jnp.exp2(one - top) for one in tops]
        total = sum(factor * one for factor, one in zip(factors, totals))
        return sum(factor * one for factor, one in zip(factors, sums)), top, total

    tails = [part[HD:, :].astype(jnp.float32) for part in parts]
    stats = [tail[8:16] for tail in tails]
    pre = add(
        [one[0:1] + one[1:2] + one[2:3] for one in stats],
        [one[3:4] + one[4:5] + one[5:6] for one in stats],
        [part[:HD, :].astype(jnp.float32) for part in parts],
    )
    dec = []
    for b in range(DEC):
        lanes = slice(b * HD, (b + 1) * HD)
        stats = [tail[14:15, lanes] for tail in tails]

        def column(stat, places):
            mask = functools.reduce(jnp.logical_or, [in_lanes(n) for n in places])
            return jnp.sum(jnp.where(mask, stat, 0.0), axis=1, keepdims=True)

        dec.append(
            add(
                [column(stat, range(3)) for stat in stats],
                [column(stat, range(3, 6)) for stat in stats],
                [tail[:8, lanes] for tail in tails],
            )
        )
    return pre, dec


def join_some_kernel(*refs):
    parts, outs = refs[:ACROSS], refs[ACROSS:]
    section, _, fast = place_of_device()
    for by, out in zip(FAST_ORDER, outs):
        target = moved(fast, by)
        pre, dec = joined([part.at[target] for part in parts])
        out[...] = packed(*pre, dec)


def join_some(parts):
    return pl.pallas_call(
        join_some_kernel,
        in_specs=[pl.BlockSpec(memory_space=pltpu.VMEM)] * ACROSS,
        out_specs=[pl.BlockSpec(memory_space=pltpu.VMEM)] * ACROSS,
        out_shape=[jax.ShapeDtypeStruct((ROWS, LANES // 2), jnp.bfloat16)] * ACROSS,
        compiler_params=pltpu.CompilerParams(vmem_limit_bytes=32 * 1024 * 1024),
        name="join_some",
    )(*parts)


def join_last_kernel(*refs):
    (acc, _, total), dec = joined(refs[:-1])
    result = (acc / total).T
    rows = []
    for dec_acc, _, dec_total in dec:
        one = dec_acc / dec_total
        rows.append(jnp.concatenate([one[g : g + 1] for g in range(HALF)], 1))
    rows.append(jnp.concatenate([result[g * PRE : (g + 1) * PRE] for g in range(HALF)], 1))
    refs[-1][...] = jnp.concatenate(rows, 0).astype(jnp.bfloat16)


def join_last(parts):
    return pl.pallas_call(
        join_last_kernel,
        in_specs=[pl.BlockSpec(memory_space=pltpu.VMEM)] * ACROSS,
        out_specs=pl.BlockSpec(memory_space=pltpu.VMEM),
        out_shape=jax.ShapeDtypeStruct((DEC + PRE, HALF * HD), jnp.bfloat16),
        compiler_params=pltpu.CompilerParams(vmem_limit_bytes=32 * 1024 * 1024),
        name="join_last",
    )(*parts)


def sent(value, step):
    sections = lax.axis_size("pipe")
    pairs = []
    for section in range(sections):
        by_section, by_slow, by_fast = step(section)
        to_section = (section + by_section) % sections
        for slow in range(ACROSS):
            for fast in range(ACROSS):
                to = ((slow + by_slow) % ACROSS) * ACROSS + (fast + by_fast) % ACROSS
                here = (section * ACROSS + slow) * ACROSS + fast
                pairs.append((here, to_section * ACROSS * ACROSS + to))
    return lax.ppermute(value, ("pipe", "tensor"), pairs)


ORDER = ((2, 2), (3, 1), (1, 3), (0, 0))
FAST_ORDER = (2, 1, 3, 0)


def on_device(queries, cache_k, cache_v, dec_lengths, pre_starts):
    sources = [
        pltpu.with_memory_space_constraint(one, pltpu.HBM) for one in (queries[0], cache_k[0], cache_v[0])
    ]
    lengths = pltpu.with_memory_space_constraint(dec_lengths, pltpu.HBM)
    held, parts = [], []
    for shift, after in zip(ORDER, (*ORDER[1:], None)):
        part, lengths, held = attend(shift, after, pre_starts, lengths, held, sources)
        if shift != (0, 0):
            part = sent(part, lambda section, shift=shift: (0, shift[section % 2], 0))
        parts.append(part)
    shares = join_some(parts)
    shares = [sent(share, lambda section, by=by: (1, 0, by)) for by, share in zip(FAST_ORDER, shares)]
    return join_last(shares)[None]


def solution(mesh):
    in_specs = (
        P(("dp", "pipe"), None, None),
        P(("dp", "pipe"), None, "tensor", None),
        P(("dp", "pipe"), None, "tensor", None),
        P(("dp", "pipe"), None),
        P(("dp", "pipe")),
    )
    out_specs = P(("dp", "pipe"), None, "tensor")
    return jax.shard_map(
        on_device, mesh=mesh, in_specs=in_specs, out_specs=out_specs, check_vma=False
    )
```

```python
import functools
import math

import jax
import jax.numpy as jnp
from jax import lax
from jax.experimental import pallas as pl
from jax.experimental.pallas import tpu as pltpu
from jax.sharding import PartitionSpec as P

HQ = 128
KVH = 8
HD = 128
GROUP = HQ // KVH
ACROSS = 4
HALF = GROUP // 2
DEC = 2
PRE = 32
LANES = GROUP * PRE
PAIR = 2
QK_TILE = 512
PV_TILE = 1024
ROWS = 144
SCALE = math.log2(math.e) / math.sqrt(HD)
DEAD = -1e30
FLOOR = -1e29
VMEM_LIMIT = 36 * 1024 * 1024
FETCHED = ("q", "k", "K", "n", "v", "k0", "v0", "k1", "v1")
FIRST_SCHEDULE = "A0A1AA" "xBBa0Ba0B0" "Wb01b01" "111"
SCHEDULE = "A0A1AA" "Ba0Ba0B0B" "b01b01" "111"


def three_parts(x):
    first = x.astype(jnp.bfloat16).astype(jnp.float32)
    rest = x - first
    second = rest.astype(jnp.bfloat16).astype(jnp.float32)
    return first, second, rest - second


def nt_dot(a, b):
    return lax.dot_general(a, b, (((1,), (1,)), ((), ())), preferred_element_type=jnp.float32)


def tn_dot(a, b):
    return lax.dot_general(a, b, (((0,), (0,)), ((), ())), preferred_element_type=jnp.float32)


def scores_of(keys, query, s_ref, limit):
    local_len = keys.shape[0]
    top = jnp.full((1, LANES), FLOOR, jnp.float32)
    for at in range(0, local_len, QK_TILE):
        block = keys[at : at + QK_TILE]
        scores = nt_dot(jnp.concatenate([block, block], 1), query)
        if limit is not None:
            place = lax.broadcasted_iota(jnp.int32, (QK_TILE, LANES), 0) + at
            scores = jnp.where(place <= limit, scores, DEAD)
        s_ref[at : at + QK_TILE] = scores
        top = jnp.maximum(top, jnp.max(scores, axis=0, keepdims=True))
        yield top


def weighted_of(values, s_ref, top_of):
    local_len = values.shape[0]
    top = top_of()
    acc = None
    for at in range(0, local_len, PV_TILE):
        weights = jnp.exp2(s_ref[at : at + PV_TILE] - top).astype(jnp.bfloat16)
        block = jnp.concatenate(
            [values[at : at + PV_TILE].T, jnp.ones((16, PV_TILE), jnp.bfloat16)], 0
        )
        part = jnp.dot(block, weights, preferred_element_type=jnp.float32)
        acc = part if acc is None else acc + part
        yield acc


def decode_of(b, rows, k_ref, v_ref, length):
    local_len = k_ref.shape[1]
    blank = jnp.zeros((GROUP, HD), jnp.float32)
    query = []
    for n in range(PAIR):
        part = jnp.concatenate(
            [rows[b : b + 1, (n * GROUP + g) * HD : (n * GROUP + g + 1) * HD] for g in range(GROUP)], 0
        )
        query.append(jnp.concatenate([part if n == m else blank for m in range(PAIR)], 1))
    query = jnp.concatenate(query, 0).astype(jnp.bfloat16)
    yield
    scores = nt_dot(query, k_ref[b]) * SCALE
    yield
    place = lax.broadcasted_iota(jnp.int32, (GROUP * PAIR, local_len), 1)
    scores = jnp.where(place < length, scores, DEAD)
    top = jnp.maximum(jnp.max(scores, axis=1, keepdims=True), FLOOR)
    yield
    weights = jnp.exp2(scores - top)
    total = jnp.sum(weights, axis=1, keepdims=True)
    yield
    both = jnp.dot(weights.astype(jnp.bfloat16), v_ref[b], preferred_element_type=jnp.float32)
    yield
    weighted = jnp.concatenate(
        [both[n * GROUP : (n + 1) * GROUP, n * HD : (n + 1) * HD] for n in range(PAIR)], 0
    )
    yield weighted, top, total


def place_of_device():
    place = lax.axis_index("tensor")
    return lax.axis_index("pipe"), place // ACROSS, place % ACROSS


def moved(here, by):
    return lax.rem(here + by, ACROSS)


def fetches(shift, sources, targets, sems, by_head=False):
    section, slow, _ = place_of_device()
    pair = moved(slow, jnp.where(section == 0, shift[0], shift[1]))
    q_hbm, k_hbm, v_hbm = sources
    q_ref, k_ref, v_ref = targets

    def columns(count):
        return pl.ds(pl.multiple_of(pair * count, count), count)

    moves = {"q": (q_hbm.at[:, columns(PAIR * GROUP * HD)], q_ref)}
    for name, sequence in (("", DEC), *((str(b), b) for b in range(DEC))):
        for kind, hbm, ref in (("k", k_hbm, k_ref), ("v", v_hbm, v_ref)):
            moves[kind + name] = (hbm.at[sequence, :, columns(PAIR * HD)], ref.at[sequence])
    if by_head:
        for n, name in enumerate(("k", "K")):
            head = pl.ds(pl.multiple_of((pair * PAIR + n) * HD, HD), HD)
            moves[name] = (k_hbm.at[DEC, :, head], k_ref.at[DEC, :, n * HD : (n + 1) * HD])
    return {
        name: pltpu.make_async_copy(*move, sems.at[n]) for n, (name, move) in enumerate(moves.items())
    }


def attend_kernel(shift, after, *refs):
    refs = list(refs)

    def take(count):
        return [refs.pop(0) for _ in range(count)]

    first = shift == ORDER[0]
    (starts,) = take(1)
    if first:
        (lengths_hbm,) = take(1)
    else:
        (lengths_ref,) = take(1)
        held = take(3)
    sources = take(3) if first or after is not None else None
    (out_ref,) = take(1)
    if first:
        (lengths_ref,) = take(1)
    coming = take(3) if after is not None else None
    s_first, s_second, sems, later_sems = take(4)
    if first:
        lengths, *held = take(4)
    q_ref, k_ref, v_ref = held
    local_len = k_ref.shape[1]
    offset = lax.axis_index("tensor") * local_len

    waiting = {}
    if first:
        waiting = fetches(shift, sources, held, sems, True)
        waiting["n"] = pltpu.make_async_copy(lengths_hbm, lengths, sems.at[len(waiting)])
        for name in FETCHED:
            waiting[name].start()
    later = fetches(after, sources, coming, later_sems) if after is not None else {}

    def start_later():
        for copy in later.values():
            copy.start()

    if not first:
        start_later()

    @pl.when(starts[0] >= 0)
    def _():
        def wait(names):
            for name in names:
                if name in waiting:
                    waiting.pop(name).wait()

        wait(("q",))
        rows = q_ref[...].astype(jnp.float32)
        pre_rows = rows[DEC:] * SCALE
        queries = []
        for n in range(PAIR):
            query = jnp.concatenate(
                [pre_rows[:, (n * GROUP + g) * HD : (n * GROUP + g + 1) * HD] for g in range(GROUP)], 0
            )
            high = query.astype(jnp.bfloat16)
            low = (query - high.astype(jnp.float32)).astype(jnp.bfloat16)
            queries.append(jnp.concatenate([high, low], 1))
        wait(("n", "k"))
        if first:
            start_later()
        token = lax.broadcasted_iota(jnp.int32, (1, LANES), 1) % PRE
        limit = starts[0] + token - offset
        if first:
            row = lax.broadcasted_iota(jnp.int32, lengths_ref.shape, 0)
            lengths_ref[...] = functools.reduce(
                lambda rest, b: jnp.where(row == b, lengths[0, b], rest), range(DEC), jnp.zeros_like(row)
            )

        def keys(n):
            return k_ref.at[DEC, :, n * HD : (n + 1) * HD]

        def values(n):
            return v_ref.at[DEC, :, n * HD : (n + 1) * HD]

        last = {}
        streams = {
            "A": scores_of(keys(0), queries[0], s_first, limit),
            "B": scores_of(keys(1), queries[1], s_second, limit),
            "a": weighted_of(values(0), s_first, lambda: last["A"]),
            "b": weighted_of(values(1), s_second, lambda: last["B"]),
        }
        for b in range(DEC):
            length = lengths[0, b] if first else lengths_ref[b : b + 1, 0:1]
            streams[str(b)] = decode_of(b, rows, k_ref, v_ref, length - offset)
        for name in FIRST_SCHEDULE if first else SCHEDULE:
            if name == "x":
                wait(("K", "v", "k0"))
            elif name == "W":
                wait(list(waiting))
            else:
                last[name] = next(streams[name])
        dec_first, dec_second = last["0"], last["1"]
        top_first, acc_first, top_second, acc_second = (last[name] for name in "AaBb")
        for n, (top, acc) in enumerate(((top_first, acc_first), (top_second, acc_second))):
            for j in range(2):
                heads = slice(n * GROUP + j * HALF, n * GROUP + (j + 1) * HALF)
                lanes = slice(j * LANES // 2, (j + 1) * LANES // 2)
                out_ref[2 * n + j] = packed(
                    acc[:HD, lanes],
                    top[:, lanes],
                    acc[HD : HD + 1, lanes],
                    [[part[heads] for part in one] for one in (dec_first, dec_second)],
                )
    for copy in later.values():
        copy.wait()


def packed(acc, top, total, dec):
    dec_stats = []
    for _, dec_top, dec_total in dec:
        parts = [*three_parts(dec_top), *three_parts(dec_total)]
        stats = sum(jnp.where(in_lanes(n), part, 0.0) for n, part in enumerate(parts))
        dec_stats.append(jnp.sum(stats, axis=0, keepdims=True))
    return jnp.concatenate(
        [
            acc,
            jnp.concatenate([one[0] for one in dec], 1),
            *three_parts(top),
            *three_parts(total),
            jnp.concatenate(dec_stats, 1),
            jnp.zeros((1, LANES // 2), jnp.float32),
        ],
        0,
    ).astype(jnp.bfloat16)


def in_lanes(n):
    row = lax.broadcasted_iota(jnp.int32, (HALF, HD), 0)
    return lax.broadcasted_iota(jnp.int32, (HALF, HD), 1) == n * HALF + row


def attend(shift, after, starts, lengths, held, sources):
    first = shift == ORDER[0]
    queries, cache_k, _ = sources
    rows = queries.shape[0]
    sequences, local_len, _ = cache_k.shape
    operands = [
        ((rows, PAIR * GROUP * HD), queries.dtype),
        ((sequences, local_len, PAIR * HD), cache_k.dtype),
        ((sequences, local_len, PAIR * HD), cache_k.dtype),
    ]
    args = [starts, lengths, *held]
    in_specs = [pl.BlockSpec(memory_space=pltpu.SMEM)]
    in_specs += [pl.BlockSpec(memory_space=pl.ANY if first else pltpu.VMEM)] * (1 + len(held))
    if first or after is not None:
        args += sources
        in_specs += [pl.BlockSpec(memory_space=pl.ANY)] * 3
    outs = [pltpu.VMEM((ACROSS, ROWS, LANES // 2), jnp.bfloat16)]
    if first:
        outs.append(pltpu.VMEM((8, HD), jnp.int32))
    if after is not None:
        outs += [pltpu.VMEM(*operand) for operand in operands]
    scratch = [
        pltpu.VMEM((local_len, LANES), jnp.float32),
        pltpu.VMEM((local_len, LANES), jnp.float32),
        pltpu.SemaphoreType.DMA((2 * sequences + 3,)),
        pltpu.SemaphoreType.DMA((2 * sequences + 3,)),
    ]
    if first:
        scratch.append(pltpu.SMEM(lengths.shape, jnp.int32))
        scratch += [pltpu.VMEM(*operand) for operand in operands]
    part, *rest = pl.pallas_call(
        functools.partial(attend_kernel, shift, after),
        in_specs=in_specs,
        out_specs=[pl.BlockSpec(memory_space=pltpu.VMEM)] * len(outs),
        out_shape=outs,
        scratch_shapes=scratch,
        compiler_params=pltpu.CompilerParams(vmem_limit_bytes=VMEM_LIMIT),
        cost_estimate=pl.CostEstimate(
            flops=4 * PAIR * GROUP * HD * (PRE + DEC) * local_len,
            bytes_accessed=4 * sequences * local_len * PAIR * HD,
            transcendentals=PAIR * GROUP * (PRE + DEC) * local_len,
        ),
        name="attend",
    )(*args)
    if first:
        lengths, *rest = rest
    return part, lengths, rest


def joined(parts):
    def add(tops, totals, sums):
        top = functools.reduce(jnp.maximum, tops)
        factors = [jnp.exp2(one - top) for one in tops]
        total = sum(factor * one for factor, one in zip(factors, totals))
        return sum(factor * one for factor, one in zip(factors, sums)), top, total

    tails = [part[HD:, :].astype(jnp.float32) for part in parts]
    stats = [tail[8:16] for tail in tails]
    pre = add(
        [one[0:1] + one[1:2] + one[2:3] for one in stats],
        [one[3:4] + one[4:5] + one[5:6] for one in stats],
        [part[:HD, :].astype(jnp.float32) for part in parts],
    )
    dec = []
    for b in range(DEC):
        lanes = slice(b * HD, (b + 1) * HD)
        stats = [tail[14:15, lanes] for tail in tails]

        def column(stat, places):
            mask = functools.reduce(jnp.logical_or, [in_lanes(n) for n in places])
            return jnp.sum(jnp.where(mask, stat, 0.0), axis=1, keepdims=True)

        dec.append(
            add(
                [column(stat, range(3)) for stat in stats],
                [column(stat, range(3, 6)) for stat in stats],
                [tail[:8, lanes] for tail in tails],
            )
        )
    return pre, dec


def join_some_kernel(*refs):
    parts, outs = refs[:ACROSS], refs[ACROSS:]
    section, _, fast = place_of_device()
    for by, out in zip(FAST_ORDER, outs):
        target = moved(fast, by)
        pre, dec = joined([part.at[target] for part in parts])
        out[...] = packed(*pre, dec)


def join_some(parts):
    return pl.pallas_call(
        join_some_kernel,
        in_specs=[pl.BlockSpec(memory_space=pltpu.VMEM)] * ACROSS,
        out_specs=[pl.BlockSpec(memory_space=pltpu.VMEM)] * ACROSS,
        out_shape=[jax.ShapeDtypeStruct((ROWS, LANES // 2), jnp.bfloat16)] * ACROSS,
        compiler_params=pltpu.CompilerParams(vmem_limit_bytes=32 * 1024 * 1024),
        name="join_some",
    )(*parts)


def join_last_kernel(*refs):
    (acc, _, total), dec = joined(refs[:-1])
    result = (acc / total).T
    rows = []
    for dec_acc, _, dec_total in dec:
        one = dec_acc / dec_total
        rows.append(jnp.concatenate([one[g : g + 1] for g in range(HALF)], 1))
    rows.append(jnp.concatenate([result[g * PRE : (g + 1) * PRE] for g in range(HALF)], 1))
    refs[-1][...] = jnp.concatenate(rows, 0).astype(jnp.bfloat16)


def join_last(parts):
    return pl.pallas_call(
        join_last_kernel,
        in_specs=[pl.BlockSpec(memory_space=pltpu.VMEM)] * ACROSS,
        out_specs=pl.BlockSpec(memory_space=pltpu.VMEM),
        out_shape=jax.ShapeDtypeStruct((DEC + PRE, HALF * HD), jnp.bfloat16),
        compiler_params=pltpu.CompilerParams(vmem_limit_bytes=32 * 1024 * 1024),
        name="join_last",
    )(*parts)


def sent(value, step):
    sections = lax.axis_size("pipe")
    pairs = []
    for section in range(sections):
        by_section, by_slow, by_fast = step(section)
        to_section = (section + by_section) % sections
        for slow in range(ACROSS):
            for fast in range(ACROSS):
                to = ((slow + by_slow) % ACROSS) * ACROSS + (fast + by_fast) % ACROSS
                here = (section * ACROSS + slow) * ACROSS + fast
                pairs.append((here, to_section * ACROSS * ACROSS + to))
    return lax.ppermute(value, ("pipe", "tensor"), pairs)


ORDER = ((2, 2), (3, 1), (1, 3), (0, 0))
FAST_ORDER = (2, 1, 3, 0)


def on_device(queries, cache_k, cache_v, dec_lengths, pre_starts):
    sources = [
        pltpu.with_memory_space_constraint(one, pltpu.HBM) for one in (queries[0], cache_k[0], cache_v[0])
    ]
    lengths = pltpu.with_memory_space_constraint(dec_lengths, pltpu.HBM)
    held, parts = [], []
    for shift, after in zip(ORDER, (*ORDER[1:], None)):
        part, lengths, held = attend(shift, after, pre_starts, lengths, held, sources)
        if shift != (0, 0):
            part = sent(part, lambda section, shift=shift: (0, shift[section % 2], 0))
        parts.append(part)
    shares = join_some(parts)
    shares = [sent(share, lambda section, by=by: (1, 0, by)) for by, share in zip(FAST_ORDER, shares)]
    return join_last(shares)[None]


def solution(mesh):
    in_specs = (
        P(("dp", "pipe"), None, None),
        P(("dp", "pipe"), None, "tensor", None),
        P(("dp", "pipe"), None, "tensor", None),
        P(("dp", "pipe"), None),
        P(("dp", "pipe")),
    )
    out_specs = P(("dp", "pipe"), None, "tensor")
    return jax.shard_map(
        on_device, mesh=mesh, in_specs=in_specs, out_specs=out_specs, check_vma=False
    )
```

```python
import functools
import math

import jax
import jax.numpy as jnp
from jax import lax
from jax.experimental import pallas as pl
from jax.experimental.pallas import tpu as pltpu
from jax.sharding import PartitionSpec as P

HQ = 128
KVH = 8
HD = 128
GROUP = HQ // KVH
ACROSS = 4
HALF = GROUP // 2
DEC = 2
PRE = 32
LANES = GROUP * PRE
PAIR = 2
QK_TILE = 512
PV_TILE = 1024
ROWS = 144
SCALE = math.log2(math.e) / math.sqrt(HD)
DEAD = -1e30
FLOOR = -1e29
VMEM_LIMIT = 36 * 1024 * 1024
FETCHED = ("q", "k", "K", "n", "v", "k0", "v0", "k1", "v1")
FIRST_SCHEDULE = "A0A1AA" "xBBa0Ba0B0" "Wb01b01" "111"
SCHEDULE = "A0A1AA" "Ba0Ba0B0B" "b01b01" "111"


def three_parts(x):
    first = x.astype(jnp.bfloat16).astype(jnp.float32)
    rest = x - first
    second = rest.astype(jnp.bfloat16).astype(jnp.float32)
    return first, second, rest - second


def nt_dot(a, b):
    return lax.dot_general(a, b, (((1,), (1,)), ((), ())), preferred_element_type=jnp.float32)


def tn_dot(a, b):
    return lax.dot_general(a, b, (((0,), (0,)), ((), ())), preferred_element_type=jnp.float32)


def scores_of(keys, query, s_ref, limit):
    local_len = keys.shape[0]
    top = jnp.full((1, LANES), FLOOR, jnp.float32)
    for at in range(0, local_len, QK_TILE):
        block = keys[at : at + QK_TILE]
        scores = nt_dot(jnp.concatenate([block, block], 1), query)
        if limit is not None:
            place = lax.broadcasted_iota(jnp.int32, (QK_TILE, LANES), 0) + at
            scores = jnp.where(place <= limit, scores, DEAD)
        s_ref[at : at + QK_TILE] = scores
        top = jnp.maximum(top, jnp.max(scores, axis=0, keepdims=True))
        yield top


def weighted_of(values, s_ref, top_of):
    local_len = values.shape[0]
    top = top_of()
    acc = None
    for at in range(0, local_len, PV_TILE):
        weights = jnp.exp2(s_ref[at : at + PV_TILE] - top).astype(jnp.bfloat16)
        block = jnp.concatenate(
            [values[at : at + PV_TILE].T, jnp.ones((16, PV_TILE), jnp.bfloat16)], 0
        )
        part = jnp.dot(block, weights, preferred_element_type=jnp.float32)
        acc = part if acc is None else acc + part
        yield acc


def decode_of(b, rows, k_ref, v_ref, length):
    local_len = k_ref.shape[1]
    blank = jnp.zeros((GROUP, HD), jnp.float32)
    query = []
    for n in range(PAIR):
        part = jnp.concatenate(
            [rows[b : b + 1, (n * GROUP + g) * HD : (n * GROUP + g + 1) * HD] for g in range(GROUP)], 0
        )
        query.append(jnp.concatenate([part if n == m else blank for m in range(PAIR)], 1))
    query = jnp.concatenate(query, 0).astype(jnp.bfloat16)
    yield
    scores = nt_dot(query, k_ref[b]) * SCALE
    yield
    place = lax.broadcasted_iota(jnp.int32, (GROUP * PAIR, local_len), 1)
    scores = jnp.where(place < length, scores, DEAD)
    top = jnp.maximum(jnp.max(scores, axis=1, keepdims=True), FLOOR)
    yield
    weights = jnp.exp2(scores - top)
    total = jnp.sum(weights, axis=1, keepdims=True)
    yield
    both = jnp.dot(weights.astype(jnp.bfloat16), v_ref[b], preferred_element_type=jnp.float32)
    yield
    weighted = jnp.concatenate(
        [both[n * GROUP : (n + 1) * GROUP, n * HD : (n + 1) * HD] for n in range(PAIR)], 0
    )
    yield weighted, top, total


def place_of_device():
    place = lax.axis_index("tensor")
    return lax.axis_index("pipe"), place // ACROSS, place % ACROSS


def moved(here, by):
    return lax.rem(here + by, ACROSS)


def fetches(shift, sources, targets, sems, by_head=False):
    section, slow, _ = place_of_device()
    pair = moved(slow, jnp.where(section == 0, shift[0], shift[1]))
    q_hbm, k_hbm, v_hbm = sources
    q_ref, k_ref, v_ref = targets

    def columns(count):
        return pl.ds(pl.multiple_of(pair * count, count), count)

    moves = {"q": (q_hbm.at[:, columns(PAIR * GROUP * HD)], q_ref)}
    for name, sequence in (("", DEC), *((str(b), b) for b in range(DEC))):
        for kind, hbm, ref in (("k", k_hbm, k_ref), ("v", v_hbm, v_ref)):
            moves[kind + name] = (hbm.at[sequence, :, columns(PAIR * HD)], ref.at[sequence])
    if by_head:
        for n, name in enumerate(("k", "K")):
            head = pl.ds(pl.multiple_of((pair * PAIR + n) * HD, HD), HD)
            moves[name] = (k_hbm.at[DEC, :, head], k_ref.at[DEC, :, n * HD : (n + 1) * HD])
    return {
        name: pltpu.make_async_copy(*move, sems.at[n]) for n, (name, move) in enumerate(moves.items())
    }


def attend_kernel(shift, after, *refs):
    refs = list(refs)

    def take(count):
        return [refs.pop(0) for _ in range(count)]

    first = shift == ORDER[0]
    (starts,) = take(1)
    if first:
        (lengths_hbm,) = take(1)
    else:
        (lengths_ref,) = take(1)
        held = take(3)
    sources = take(3) if first or after is not None else None
    (out_ref,) = take(1)
    if first:
        (lengths_ref,) = take(1)
    coming = take(3) if after is not None else None
    s_first, s_second, sems, later_sems = take(4)
    if first:
        lengths, *held = take(4)
    q_ref, k_ref, v_ref = held
    local_len = k_ref.shape[1]
    offset = lax.axis_index("tensor") * local_len

    waiting = {}
    if first:
        waiting = fetches(shift, sources, held, sems, True)
        waiting["n"] = pltpu.make_async_copy(lengths_hbm, lengths, sems.at[len(waiting)])
        for name in FETCHED:
            waiting[name].start()
    later = fetches(after, sources, coming, later_sems) if after is not None else {}

    def start_later():
        for copy in later.values():
            copy.start()

    if not first:
        start_later()

    @pl.when(starts[0] >= 0)
    def _():
        def wait(names):
            for name in names:
                if name in waiting:
                    waiting.pop(name).wait()

        wait(("q",))
        rows = q_ref[...].astype(jnp.float32)
        pre_rows = rows[DEC:] * SCALE
        queries = []
        for n in range(PAIR):
            query = jnp.concatenate(
                [pre_rows[:, (n * GROUP + g) * HD : (n * GROUP + g + 1) * HD] for g in range(GROUP)], 0
            )
            high = query.astype(jnp.bfloat16)
            low = (query - high.astype(jnp.float32)).astype(jnp.bfloat16)
            queries.append(jnp.concatenate([high, low], 1))
        wait(("n", "k"))
        if first:
            start_later()
        token = lax.broadcasted_iota(jnp.int32, (1, LANES), 1) % PRE
        limit = starts[0] + token - offset
        if first:
            row = lax.broadcasted_iota(jnp.int32, lengths_ref.shape, 0)
            lengths_ref[...] = functools.reduce(
                lambda rest, b: jnp.where(row == b, lengths[0, b], rest), range(DEC), jnp.zeros_like(row)
            )

        def keys(n):
            return k_ref.at[DEC, :, n * HD : (n + 1) * HD]

        def values(n):
            return v_ref.at[DEC, :, n * HD : (n + 1) * HD]

        last = {}
        streams = {
            "A": scores_of(keys(0), queries[0], s_first, limit),
            "B": scores_of(keys(1), queries[1], s_second, limit),
            "a": weighted_of(values(0), s_first, lambda: last["A"]),
            "b": weighted_of(values(1), s_second, lambda: last["B"]),
        }
        for b in range(DEC):
            length = lengths[0, b] if first else lengths_ref[b : b + 1, 0:1]
            streams[str(b)] = decode_of(b, rows, k_ref, v_ref, length - offset)
        for name in FIRST_SCHEDULE if first else SCHEDULE:
            if name == "x":
                wait(("K", "v", "k0"))
            elif name == "W":
                wait(list(waiting))
            else:
                last[name] = next(streams[name])
        dec_first, dec_second = last["0"], last["1"]
        top_first, acc_first, top_second, acc_second = (last[name] for name in "AaBb")
        for n, (top, acc) in enumerate(((top_first, acc_first), (top_second, acc_second))):
            for j in range(2):
                heads = slice(n * GROUP + j * HALF, n * GROUP + (j + 1) * HALF)
                lanes = slice(j * LANES // 2, (j + 1) * LANES // 2)
                out_ref[2 * n + j] = packed(
                    acc[:HD, lanes],
                    top[:, lanes],
                    acc[HD : HD + 1, lanes],
                    [[part[heads] for part in one] for one in (dec_first, dec_second)],
                )
    for copy in later.values():
        copy.wait()


def packed(acc, top, total, dec):
    dec_stats = []
    for _, dec_top, dec_total in dec:
        parts = [*three_parts(dec_top), *three_parts(dec_total)]
        stats = sum(jnp.where(in_lanes(n), part, 0.0) for n, part in enumerate(parts))
        dec_stats.append(jnp.sum(stats, axis=0, keepdims=True))
    return jnp.concatenate(
        [
            acc,
            jnp.concatenate([one[0] for one in dec], 1),
            *three_parts(top),
            *three_parts(total),
            jnp.concatenate(dec_stats, 1),
            jnp.zeros((1, LANES // 2), jnp.float32),
        ],
        0,
    ).astype(jnp.bfloat16)


def in_lanes(n):
    row = lax.broadcasted_iota(jnp.int32, (HALF, HD), 0)
    return lax.broadcasted_iota(jnp.int32, (HALF, HD), 1) == n * HALF + row


def attend(shift, after, starts, lengths, held, sources):
    first = shift == ORDER[0]
    queries, cache_k, _ = sources
    rows = queries.shape[0]
    sequences, local_len, _ = cache_k.shape
    operands = [
        ((rows, PAIR * GROUP * HD), queries.dtype),
        ((sequences, local_len, PAIR * HD), cache_k.dtype),
        ((sequences, local_len, PAIR * HD), cache_k.dtype),
    ]
    args = [starts, lengths, *held]
    in_specs = [pl.BlockSpec(memory_space=pltpu.SMEM)]
    in_specs += [pl.BlockSpec(memory_space=pl.ANY if first else pltpu.VMEM)] * (1 + len(held))
    if first or after is not None:
        args += sources
        in_specs += [pl.BlockSpec(memory_space=pl.ANY)] * 3
    outs = [pltpu.VMEM((ACROSS, ROWS, LANES // 2), jnp.bfloat16)]
    if first:
        outs.append(pltpu.VMEM((8, HD), jnp.int32))
    if after is not None:
        outs += [pltpu.VMEM(*operand) for operand in operands]
    scratch = [
        pltpu.VMEM((local_len, LANES), jnp.float32),
        pltpu.VMEM((local_len, LANES), jnp.float32),
        pltpu.SemaphoreType.DMA((2 * sequences + 3,)),
        pltpu.SemaphoreType.DMA((2 * sequences + 3,)),
    ]
    if first:
        scratch.append(pltpu.SMEM(lengths.shape, jnp.int32))
        scratch += [pltpu.VMEM(*operand) for operand in operands]
    part, *rest = pl.pallas_call(
        functools.partial(attend_kernel, shift, after),
        in_specs=in_specs,
        out_specs=[pl.BlockSpec(memory_space=pltpu.VMEM)] * len(outs),
        out_shape=outs,
        scratch_shapes=scratch,
        compiler_params=pltpu.CompilerParams(vmem_limit_bytes=VMEM_LIMIT),
        cost_estimate=pl.CostEstimate(
            flops=4 * PAIR * GROUP * HD * (PRE + DEC) * local_len,
            bytes_accessed=4 * sequences * local_len * PAIR * HD,
            transcendentals=PAIR * GROUP * (PRE + DEC) * local_len,
        ),
        name="attend",
    )(*args)
    if first:
        lengths, *rest = rest
    return part, lengths, rest


def joined(parts):
    def add(tops, totals, sums):
        top = functools.reduce(jnp.maximum, tops)
        factors = [jnp.exp2(one - top) for one in tops]
        total = sum(factor * one for factor, one in zip(factors, totals))
        return sum(factor * one for factor, one in zip(factors, sums)), top, total

    tails = [part[HD:, :].astype(jnp.float32) for part in parts]
    stats = [tail[8:16] for tail in tails]
    pre = add(
        [one[0:1] + one[1:2] + one[2:3] for one in stats],
        [one[3:4] + one[4:5] + one[5:6] for one in stats],
        [part[:HD, :].astype(jnp.float32) for part in parts],
    )
    dec = []
    for b in range(DEC):
        lanes = slice(b * HD, (b + 1) * HD)
        stats = [tail[14:15, lanes] for tail in tails]

        def column(stat, places):
            mask = functools.reduce(jnp.logical_or, [in_lanes(n) for n in places])
            return jnp.sum(jnp.where(mask, stat, 0.0), axis=1, keepdims=True)

        dec.append(
            add(
                [column(stat, range(3)) for stat in stats],
                [column(stat, range(3, 6)) for stat in stats],
                [tail[:8, lanes] for tail in tails],
            )
        )
    return pre, dec


def join_some_kernel(*refs):
    parts, outs = refs[:ACROSS], refs[ACROSS:]
    section, _, fast = place_of_device()
    for by, out in zip(FAST_ORDER, outs):
        target = moved(fast, by)
        pre, dec = joined([part.at[target] for part in parts])
        out[...] = packed(*pre, dec)


def join_some(parts):
    return pl.pallas_call(
        join_some_kernel,
        in_specs=[pl.BlockSpec(memory_space=pltpu.VMEM)] * ACROSS,
        out_specs=[pl.BlockSpec(memory_space=pltpu.VMEM)] * ACROSS,
        out_shape=[jax.ShapeDtypeStruct((ROWS, LANES // 2), jnp.bfloat16)] * ACROSS,
        compiler_params=pltpu.CompilerParams(vmem_limit_bytes=32 * 1024 * 1024),
        name="join_some",
    )(*parts)


def join_last_kernel(*refs):
    (acc, _, total), dec = joined(refs[:-1])
    result = (acc * (1.0 / total)).T
    rows = []
    for dec_acc, _, dec_total in dec:
        one = dec_acc * (1.0 / dec_total)
        rows.append(jnp.concatenate([one[g : g + 1] for g in range(HALF)], 1))
    rows.append(jnp.concatenate([result[g * PRE : (g + 1) * PRE] for g in range(HALF)], 1))
    refs[-1][...] = jnp.concatenate(rows, 0).astype(jnp.bfloat16)


def join_last(parts):
    return pl.pallas_call(
        join_last_kernel,
        in_specs=[pl.BlockSpec(memory_space=pltpu.VMEM)] * ACROSS,
        out_specs=pl.BlockSpec(memory_space=pltpu.VMEM),
        out_shape=jax.ShapeDtypeStruct((DEC + PRE, HALF * HD), jnp.bfloat16),
        compiler_params=pltpu.CompilerParams(vmem_limit_bytes=32 * 1024 * 1024),
        name="join_last",
    )(*parts)


def sent(value, step):
    sections = lax.axis_size("pipe")
    pairs = []
    for section in range(sections):
        by_section, by_slow, by_fast = step(section)
        to_section = (section + by_section) % sections
        for slow in range(ACROSS):
            for fast in range(ACROSS):
                to = ((slow + by_slow) % ACROSS) * ACROSS + (fast + by_fast) % ACROSS
                here = (section * ACROSS + slow) * ACROSS + fast
                pairs.append((here, to_section * ACROSS * ACROSS + to))
    return lax.ppermute(value, ("pipe", "tensor"), pairs)


ORDER = ((2, 2), (3, 1), (1, 3), (0, 0))
FAST_ORDER = (2, 1, 3, 0)


def on_device(queries, cache_k, cache_v, dec_lengths, pre_starts):
    sources = [
        pltpu.with_memory_space_constraint(one, pltpu.HBM) for one in (queries[0], cache_k[0], cache_v[0])
    ]
    lengths = pltpu.with_memory_space_constraint(dec_lengths, pltpu.HBM)
    held, parts = [], []
    for shift, after in zip(ORDER, (*ORDER[1:], None)):
        part, lengths, held = attend(shift, after, pre_starts, lengths, held, sources)
        if shift != (0, 0):
            part = sent(part, lambda section, shift=shift: (0, shift[section % 2], 0))
        parts.append(part)
    shares = join_some(parts)
    shares = [sent(share, lambda section, by=by: (1, 0, by)) for by, share in zip(FAST_ORDER, shares)]
    return join_last(shares)[None]


def solution(mesh):
    in_specs = (
        P(("dp", "pipe"), None, None),
        P(("dp", "pipe"), None, "tensor", None),
        P(("dp", "pipe"), None, "tensor", None),
        P(("dp", "pipe"), None),
        P(("dp", "pipe")),
    )
    out_specs = P(("dp", "pipe"), None, "tensor")
    return jax.shard_map(
        on_device, mesh=mesh, in_specs=in_specs, out_specs=out_specs, check_vma=False
    )
```
